256 devices in a mesh: dp: 8 (over x, z_lo), pipe: 4 (over y), tensor: 8 (over z_hi, core).
Axes of the slice: x: 4, y: 4, z: 8 (z_hi: 4, z_lo: 2; z = z_hi * 2 + z_lo), core: 2. Of those that a mesh axis runs over, the one named last changes fastest.
Arguments:
- h_in: bfloat16 [2, 96, 8192], P(None, 'dp', 'tensor'), may hold values from -6 to 6
- cotangent: bfloat16 [2, 96, 8192], P(None, 'dp', 'tensor'), may hold values from -1 to 1
- w_up: bfloat16 [4, 8192, 14336], P('pipe', 'tensor', 'dp'), may hold values from -0.0625 to 0.0625
- w_down: bfloat16 [4, 14336, 8192], P('pipe', 'dp', 'tensor'), may hold values from -0.046875 to 0.046875
- a_up: bfloat16 [4, 8192, 256], P('pipe', 'tensor'), may hold values from -0.0625 to 0.0625
- b_up: bfloat16 [4, 256, 14336], P('pipe', None, 'dp'), may hold values from -0.75 to 0.75
- a_down: bfloat16 [4, 14336, 256], P('pipe', 'dp'), may hold values from -0.046875 to 0.046875
- b_down: bfloat16 [4, 256, 8192], P('pipe', None, 'tensor'), may hold values from -0.75 to 0.75
- job_ids: int32 [2, 8], replicated, may hold values from 0 to 3
- ranks: int32 [4], replicated, may hold values from 8 to 64
Outputs:
- grad_a_up: float32 [4, 8192, 256], P('pipe', 'tensor')
- grad_b_up: float32 [4, 256, 14336], P('pipe', 'tensor', 'dp')
- grad_a_down: float32 [4, 14336, 256], P('pipe', 'dp', 'tensor')
- grad_b_down: float32 [4, 256, 8192], P('pipe', None, 'tensor')
The draws below stay inside these ranges and needn't reach their ends.
All inputs are finite; a program needn't handle non-finite values.
Results may differ from the reference program's by a relative error of at most 0.025.
Values may be sent and summed in bfloat16 or wider, within the bound.
No kernel may reach another device: no remote copies, remote signals or barrier semaphores. Data moves between devices by JAX's collectives and lax.ppermute only.
A program may use at most 128 MiB of HBM per device.

```python
import jax
import jax.numpy as jnp
from jax import lax

D = 8192
FFW = 14336
RMAX = 64
JOBS = 4
MB = 2
SEQ_LEN = 12
JR = 256
SEQS = 8
TOKENS = 96
SECTIONS = 4
N_PIPE = 4


def plant(drawn, stream_key, least, top_value):
    longest = drawn.shape.index(max(drawn.shape))
    spots = []
    for shift in (0, 1):
        where = [jax.random.randint(jax.random.fold_in(stream_key, axis), (), 0, length) for axis, length in enumerate(drawn.shape)]
        where[longest] = (where[longest] + shift) % drawn.shape[longest]
        spots.append(tuple(where))
    return drawn.at[spots[0]].set(least).at[spots[1]].set(top_value)


def block_scale(own_key, dims, split, low, top_value):
    def one(position, blocks):
        draws = jax.random.uniform(jax.random.fold_in(jax.random.fold_in(own_key, 6), position), (blocks,), jnp.float32, low / len(split), top_value / len(split))
        return jnp.repeat(jnp.exp(draws), dims[position] // blocks).reshape((-1,) + (1,) * (len(dims) - position - 1))

    level = one(*split[0])
    for cut in split[1:]:
        level = level * one(*cut)
    return level


def noise(own_key, extent, deviation, bound, shards=(), kind=jnp.bfloat16):
    loudness = block_scale(own_key, extent, shards, -0.22, 0.18) if shards else 1.0
    entries = jax.random.normal(own_key, extent, jnp.float32) * deviation * loudness
    return jnp.minimum(jnp.maximum(entries, -bound), bound).astype(kind)


def setup_inputs(seed: int = 0) -> dict:
    keys = jax.random.split(jax.random.key(seed), 11)
    h_in = noise(keys[0], (MB, TOKENS, D), 1.0, 6.0, ((1, 8), (2, 8)))
    cotangent = noise(keys[1], (MB, TOKENS, D), ((MB * TOKENS) ** -0.5), 1.0, ((1, 8), (2, 8)))
    w_up = noise(keys[2], (SECTIONS, D, FFW), D ** -0.5, 0.0625, ((0, 4), (1, 8), (2, 8)))
    w_down = noise(keys[3], (SECTIONS, FFW, D), FFW ** -0.5, 0.046875, ((0, 4), (1, 8), (2, 8)))
    a_up = noise(keys[4], (SECTIONS, D, JR), D ** -0.5, 0.0625, ((0, 4), (1, 8)))
    b_up = noise(keys[5], (SECTIONS, JR, FFW), RMAX ** -0.5, 0.75, ((0, 4), (2, 8)))
    a_down = noise(keys[6], (SECTIONS, FFW, JR), FFW ** -0.5, 0.046875, ((0, 4), (1, 8)))
    b_down = noise(keys[7], (SECTIONS, JR, D), RMAX ** -0.5, 0.75, ((0, 4), (2, 8)))
    job_ids = plant(jax.random.randint(keys[8], (MB, SEQS), 0, JOBS), jax.random.fold_in(keys[8], 1), 0, JOBS - 1).astype(jnp.int32)
    ranks = plant(jax.random.randint(keys[9], (JOBS,), 8, RMAX + 1), jax.random.fold_in(keys[9], 1), 8, RMAX).astype(jnp.int32)
    return {"h_in": h_in, "cotangent": cotangent, "w_up": w_up, "w_down": w_down, "a_up": a_up, "b_up": b_up, "a_down": a_down, "b_down": b_down, "job_ids": job_ids, "ranks": ranks}


EPS = 1e-05
ALPHA = 16.0

def column_weights(ranks, lanes):
    column = jnp.arange(lanes, dtype=jnp.int32)
    col_job = column // RMAX
    picked = col_job[:, None] == jnp.arange(JOBS, dtype=jnp.int32)[None, :]
    rank_col = lax.optimization_barrier(jnp.sum(jnp.where(picked, ranks[None, :], 0), axis=1))
    scale = jnp.where(column % RMAX < rank_col, ALPHA / rank_col.astype(jnp.float32), jnp.float32(0.0))
    return (col_job, scale)

def row_mask(seq_jobs, col_job, scale):
    job_row = jnp.broadcast_to(seq_jobs[:, None], (seq_jobs.shape[0], SEQ_LEN)).reshape(-1)
    return jnp.where(job_row[:, None] == col_job[None, :], scale[None, :], jnp.float32(0.0))

def silu_grad(u):
    sig = jax.nn.sigmoid(u)
    return sig * (1.0 + u * (1.0 - sig))

def mm(left, right):
    return jnp.dot(left, right, preferred_element_type=jnp.float32)

def reference(h_in, cotangent, w_up, w_down, a_up, b_up, a_down, b_down, job_ids, ranks):
    col_job, scale = column_weights(ranks, JR)
    grad_au = [jnp.zeros((D, JR), jnp.float32) for s in range(N_PIPE)]
    grad_bu = [jnp.zeros((JR, FFW), jnp.float32) for s in range(N_PIPE)]
    grad_ad = [jnp.zeros((FFW, JR), jnp.float32) for s in range(N_PIPE)]
    grad_bd = [jnp.zeros((JR, D), jnp.float32) for s in range(N_PIPE)]
    for batch in range(MB):
        mask = row_mask(job_ids[batch], col_job, scale)
        x = h_in[batch]
        saved = []
        for s in range(N_PIPE):
            ss = lax.optimization_barrier(jnp.sum(jnp.square(x.astype(jnp.float32)), axis=1))
            rs = lax.rsqrt(ss / D + EPS)
            qb = (mm(x, a_up[s]) * mask).astype(jnp.bfloat16)
            summed = mm(x, w_up[s]) + mm(qb, b_up[s])
            u = rs[:, None] * summed
            act = jax.nn.silu(u).astype(jnp.bfloat16)
            rb = (mm(act, a_down[s]) * mask).astype(jnp.bfloat16)
            y = mm(act, w_down[s]) + mm(rb, b_down[s])
            saved.append((x, rs, summed, u, act, qb, rb))
            x = (x.astype(jnp.float32) + y).astype(jnp.bfloat16)
        g = cotangent[batch]
        for s in reversed(range(N_PIPE)):
            x, rs, summed, u, act, qb, rb = saved[s]
            grad_bd[s] = grad_bd[s] + mm(rb.T, g)
            d_rb = (mm(g, b_down[s].T) * mask).astype(jnp.bfloat16)
            grad_ad[s] = grad_ad[s] + mm(act.T, d_rb)
            d_act = mm(g, w_down[s].T) + mm(d_rb, a_down[s].T)
            d_u = d_act * silu_grad(u)
            d_sb = (d_u * rs[:, None]).astype(jnp.bfloat16)
            rowdot = lax.optimization_barrier(jnp.sum(d_u * summed, axis=1))
            grad_bu[s] = grad_bu[s] + mm(qb.T, d_sb)
            d_qb = (mm(d_sb, b_up[s].T) * mask).astype(jnp.bfloat16)
            grad_au[s] = grad_au[s] + mm(x.T, d_qb)
            d_x = g.astype(jnp.float32) + mm(d_sb, w_up[s].T) + mm(d_qb, a_up[s].T) - x.astype(jnp.float32) * (rs ** 3 / D)[:, None] * rowdot[:, None]
            g = d_x.astype(jnp.bfloat16)
    return (jnp.stack(grad_au), jnp.stack(grad_bu), jnp.stack(grad_ad), jnp.stack(grad_bd))
```

```python
import jax
import jax.numpy as jnp
from jax import lax
from jax.sharding import PartitionSpec as P

D = 8192
RMAX = 64
JOBS = 4
MB = 2
SEQ_LEN = 12
CHIPS = 4
CORES = 2

EPS = 1e-05
ALPHA = 16.0

BF = jnp.bfloat16
F32 = jnp.float32
Z_GROUPS = [[0, 2, 4, 6], [1, 3, 5, 7]]


def column_weights(ranks, lanes):
    column = jnp.arange(lanes, dtype=jnp.int32)
    col_job = column // RMAX
    picked = col_job[:, None] == jnp.arange(JOBS, dtype=jnp.int32)[None, :]
    rank_col = jnp.sum(jnp.where(picked, ranks[None, :], 0), axis=1)
    scale = jnp.where(
        column % RMAX < rank_col, ALPHA / rank_col.astype(jnp.float32), jnp.float32(0.0)
    )
    return (col_job, scale)


def silu_grad(u):
    sig = jax.nn.sigmoid(u)
    return sig * (1.0 + u * (1.0 - sig))


def mm(left, right):
    return jnp.dot(left, right, preferred_element_type=F32)


def mm_last(left, right):
    return lax.dot_general(left, right, (((1,), (1,)), ((), ())), preferred_element_type=F32)


def mm_first(left, right):
    return lax.dot_general(left, right, (((0,), (0,)), ((), ())), preferred_element_type=F32)


def core_swap(value):
    devices = lax.axis_size("tensor")
    return lax.ppermute(value, "tensor", [(i, i ^ 1) for i in range(devices)])


def z_exchange(value):
    return lax.all_to_all(value, "tensor", 0, 0, axis_index_groups=Z_GROUPS)


def dp_exchange(value):
    return lax.all_to_all(value, "dp", 0, 0)


def pipe_shift(value, step):
    n = lax.axis_size("pipe")
    return lax.ppermute(value, "pipe", [(i, (i + step) % n) for i in range(n)])


def two_terms(value):
    high = lax.reduce_precision(value, 8, 7)
    low = value - high
    return jnp.pad(jnp.stack([high, low], axis=1), ((0, 0), (0, 126)))


def sum_over_tensor(product, rows):
    half = rows.shape[0] // CORES
    got = core_swap(product(rows[half:]).astype(BF))
    part = (product(rows[:half]) + got.astype(F32)).astype(BF)
    parts = z_exchange(part.reshape(CHIPS, half // CHIPS, part.shape[1]))
    return jnp.sum(parts.astype(F32), axis=0)


def gather_tensor(value):
    first = z_exchange(value)
    first = first.reshape(CHIPS * first.shape[1], first.shape[2])
    return first, core_swap(first)


def to_chips(value):
    return jnp.broadcast_to(value[None], (CHIPS,) + value.shape)


def sum_over_dp(product, first, second):
    parts = [product(first).astype(BF), product(second).astype(BF)]
    n = lax.axis_size("dp")
    rows = first.shape[0] * CORES // n
    parts = [p.reshape(n // CORES, rows, p.shape[1]) for p in parts]
    return jnp.sum(dp_exchange(jnp.concatenate(parts, axis=0)).astype(F32), axis=0)


def gather_dp(value):
    n = lax.axis_size("dp")
    got = dp_exchange(jnp.broadcast_to(value[None], (n,) + value.shape))
    return got.reshape(n * value.shape[0], value.shape[1])


def per_device(h_in, cotangent, w_up, w_down, a_up, b_up, a_down, b_down, job_ids, ranks):
    wu, wd, au, bu, ad, bd = (w_up[0], w_down[0], a_up[0], b_up[0], a_down[0], b_down[0])
    width = h_in.shape[2]
    hidden = wu.shape[1]
    lanes = au.shape[1]
    replicas = lax.axis_size("dp")
    sections = lax.axis_size("pipe")
    section = lax.axis_index("pipe")
    place = lax.axis_index("dp")
    chip = lax.axis_index("tensor") // CORES
    core = lax.axis_index("tensor") % CORES
    rows = MB * h_in.shape[1]
    turn = core * (replicas // CORES)
    col_job, scale = column_weights(ranks, lanes)

    def mask_of(position):
        jobs = lax.dynamic_slice_in_dim(job_ids, (position + turn) % replicas, 1, 1)
        jobs = jnp.broadcast_to(jobs, (MB, SEQ_LEN)).reshape(-1)
        return jnp.where(jobs[:, None] == col_job[None, :], scale[None, :], F32(0.0))

    mask_share = mask_of(chip)
    mask_own = mask_of(place)

    both = jnp.concatenate([h_in.reshape(rows, width), cotangent.reshape(rows, width)], axis=1)
    both = gather_dp(both)
    half = both.shape[0] // CORES
    both = jnp.where(core == 0, both, jnp.concatenate([both[half:], both[:half]], axis=0))
    x_first = both[:, :width]
    g_first = both[:, width:]
    x_first_own = lax.dynamic_slice_in_dim(x_first, place * rows, rows, 0)
    g_first_own = lax.dynamic_slice_in_dim(g_first, place * rows, rows, 0)

    def up(x):
        ss = jnp.sum(jnp.square(x.astype(F32)), axis=1)
        return jnp.concatenate([mm(x, wu), mm(x, au), two_terms(ss)], axis=1)

    def up_back(g):
        return jnp.concatenate([mm_last(g, wd), mm_last(g, bd)], axis=1)

    def activate(summed):
        rs = lax.rsqrt((summed[:, hidden + lanes] + summed[:, hidden + lanes + 1]) / D + EPS)
        qb = (summed[:, hidden : hidden + lanes] * mask_share).astype(BF)
        pre = summed[:, :hidden] + mm(qb, bu)
        u = rs[:, None] * pre
        return rs, qb, pre, u, jax.nn.silu(u).astype(BF)

    def down(act):
        return jnp.concatenate([mm(act, wd), mm(act, ad)], axis=1)

    x_own, x = x_first_own, x_first
    for tick in range(sections - 1):
        with jax.named_scope("forward"):
            act = activate(sum_over_tensor(up, x))[-1]
            first, second = gather_tensor(to_chips(act))
            y = sum_over_dp(down, first, second)
            rb = (y[:, width:] * mask_own).astype(BF)
            h_next = (x_own.astype(F32) + y[:, :width] + mm(rb, bd)).astype(BF)
            x_own = jnp.where(section == 0, x_first_own, pipe_shift(h_next, 1))
            x = gather_dp(x_own)

    with jax.named_scope("turn"):

        def up_both(pair):
            return jnp.concatenate([up(pair[:, :width]), up_back(pair[:, width:])], axis=1)

        summed = sum_over_tensor(up_both, jnp.concatenate([x, g_first], axis=1))
        split = hidden + lanes + 128
        rs, qb, pre, u, act = activate(summed[:, :split])
        slope = silu_grad(u)
        d_sum = summed[:, split:]

    def hidden_grads(d_sum):
        d_rb = (d_sum[:, hidden:] * mask_share).astype(BF)
        d_u = (d_sum[:, :hidden] + mm_last(d_rb, ad)) * slope
        return d_rb, d_u, (d_u * rs[:, None]).astype(BF)

    g_own, g = g_first_own, g_first
    for tick in range(sections - 1):
        with jax.named_scope("backward"):
            d_rb, d_u, d_sb = hidden_grads(d_sum)
            factor = (rs**3 / D) * jnp.sum(d_u * pre, axis=1)
            sent = jnp.concatenate([d_sb, two_terms(factor).astype(BF)], axis=1)
            first, second = gather_tensor(to_chips(sent))

            def back(both):
                block, inputs = both[:, : hidden + 128], both[:, hidden + 128 :]
                d_s = block[:, :hidden]
                factors = block[:, hidden : hidden + 2].astype(F32)
                factors = (factors[:, 0] + factors[:, 1])[:, None]
                d_x = mm_last(d_s, wu) - inputs.astype(F32) * factors
                return jnp.concatenate([d_x, mm_last(d_s, bu)], axis=1)

            half = x.shape[0] // CORES
            d = sum_over_dp(
                back,
                jnp.concatenate([first, x[:half]], axis=1),
                jnp.concatenate([second, x[half:]], axis=1),
            )
            d_qb = (d[:, width:] * mask_own).astype(BF)
            d_x = (g_own.astype(F32) + d[:, :width] + mm_last(d_qb, au)).astype(BF)
            g_own = jnp.where(section == sections - 1, g_first_own, pipe_shift(d_x, -1))
            g = gather_dp(g_own)
            d_sum = sum_over_tensor(up_back, g)

    with jax.named_scope("last"):
        d_rb, d_u, d_sb = hidden_grads(d_sum)

        def by_chip(value):
            return jnp.swapaxes(value.reshape(value.shape[0], CHIPS, lanes // CHIPS), 0, 1)

        sent = [to_chips(d_sb), to_chips(act), by_chip(qb), by_chip(d_rb)]
        first, second = gather_tensor(jnp.concatenate(sent, axis=2))

        def adapters(block):
            d_s, a = block[:, :hidden], block[:, hidden : 2 * hidden]
            return jnp.concatenate([mm_last(d_s, bu), mm(a, ad)], axis=1)

        sums = sum_over_dp(adapters, first, second)
        sums = (sums * jnp.concatenate([mask_own, mask_own], axis=1)).astype(BF)
        gathered = gather_dp(sums)
        d_qb, rb = gathered[:, :lanes], gathered[:, lanes:]
        grad_au = mm_first(x, d_qb)
        grad_bd = mm_first(rb, g)
        whole = jnp.concatenate([first, second], axis=0)
        d_sb, act = whole[:, :hidden], whole[:, hidden : 2 * hidden]
        group = lanes // CHIPS
        piece = group // CORES
        qb = whole[:, 2 * hidden : 2 * hidden + group]
        d_rb = whole[:, 2 * hidden + group :]
        grad_bu = lax.dynamic_slice_in_dim(mm_first(qb, d_sb), core * piece, piece, 0)
        grad_ad = mm_first(act, d_rb)
        grad_ad = jnp.where(core == 0, grad_ad[:, :piece], grad_ad[:, piece:])
    return (grad_au[None], grad_bu[None], grad_ad[None], grad_bd[None])


def solution(mesh):
    in_specs = (
        P(None, "dp", "tensor"),
        P(None, "dp", "tensor"),
        P("pipe", "tensor", "dp"),
        P("pipe", "dp", "tensor"),
        P("pipe", "tensor", None),
        P("pipe", None, "dp"),
        P("pipe", "dp", None),
        P("pipe", None, "tensor"),
        P(),
        P(),
    )
    out_specs = (
        P("pipe", "tensor", None),
        P("pipe", "tensor", "dp"),
        P("pipe", "dp", "tensor"),
        P("pipe", None, "tensor"),
    )
    return jax.shard_map(
        per_device, mesh=mesh, in_specs=in_specs, out_specs=out_specs, check_vma=False
    )
```

```python
import jax
import jax.numpy as jnp
from jax import lax
from jax.experimental import pallas as pl
from jax.experimental.pallas import tpu as pltpu
from jax.sharding import PartitionSpec as P

D = 8192
RMAX = 64
JOBS = 4
MB = 2
SEQ_LEN = 12
CHIPS = 4
CORES = 2
VMEM_LIMIT = 12 * 2**20

EPS = 1e-05
ALPHA = 16.0

BF = jnp.bfloat16
F32 = jnp.float32
Z_GROUPS = [[0, 2, 4, 6], [1, 3, 5, 7]]


def column_weights(ranks, lanes):
    column = jnp.arange(lanes, dtype=jnp.int32)
    col_job = column // RMAX
    picked = col_job[:, None] == jnp.arange(JOBS, dtype=jnp.int32)[None, :]
    rank_col = jnp.sum(jnp.where(picked, ranks[None, :], 0), axis=1)
    scale = jnp.where(
        column % RMAX < rank_col, ALPHA / rank_col.astype(jnp.float32), jnp.float32(0.0)
    )
    return (col_job, scale)


def silu_grad(u):
    sig = jax.nn.sigmoid(u)
    return sig * (1.0 + u * (1.0 - sig))


def mm(left, right):
    return jnp.dot(left, right, preferred_element_type=F32)


def mm_last(left, right):
    return lax.dot_general(left, right, (((1,), (1,)), ((), ())), preferred_element_type=F32)


def mm_first(left, right):
    return lax.dot_general(left, right, (((0,), (0,)), ((), ())), preferred_element_type=F32)


def core_swap(value):
    devices = lax.axis_size("tensor")
    return lax.ppermute(value, "tensor", [(i, i ^ 1) for i in range(devices)])


def z_exchange(value):
    return lax.all_to_all(value, "tensor", 0, 0, axis_index_groups=Z_GROUPS)


def dp_exchange(value):
    return lax.all_to_all(value, "dp", 0, 0)


def pipe_shift(value, step):
    n = lax.axis_size("pipe")
    return lax.ppermute(value, "pipe", [(i, (i + step) % n) for i in range(n)])


def blocks(ref, start=0, step=1):
    picked = [ref[i].astype(F32) for i in range(start, ref.shape[0], step)]
    return jnp.concatenate(picked, axis=0).astype(BF)


def folded(adapter, mine):
    kept = adapter * mine
    fold = kept.shape[1] // 2
    return kept[:, :fold] + kept[:, fold:]


def unfolded(value, mask):
    return (jnp.concatenate([value, value], axis=1) * mask).astype(BF)


def tiles(width, size=256):
    return [(n, min(n + size, width)) for n in range(0, width, size)]


def put(out, picks, start, value):
    rows = out.shape[1]
    stop = start + value.shape[1]
    for p, i in enumerate(picks):
        out[i, :, start:stop] = value[p * rows : (p + 1) * rows].astype(BF)


def up_part(x_ref, mine, high, low, wu, wu2, au, au2, out, picks):
    x, x2 = blocks(x_ref, 0, 2), blocks(x_ref, 1, 2)
    hidden = wu.shape[1]
    for n, m in tiles(hidden):
        put(out, picks, n, mm(x, wu[:, n:m]) + mm(x2, wu2[:, n:m]))
    square = jnp.square(x.astype(F32)) + jnp.square(x2.astype(F32))
    ss = jnp.sum(square, axis=1, keepdims=True)
    top = ss.astype(BF).astype(F32)
    adapter = folded(mm(x, au[...]) + mm(x2, au2[...]), mine[...])
    put(out, picks, hidden, adapter + high[...] * top + low[...] * (ss - top))


def up_back_part(g_ref, mine, wd, wd2, bd, bd2, out, picks):
    g, g2 = blocks(g_ref, 0, 2), blocks(g_ref, 1, 2)
    hidden = wd.shape[0]
    for n, m in tiles(hidden):
        put(out, picks, n, mm_last(g, wd[n:m]) + mm_last(g2, wd2[n:m]))
    adapter = mm_last(g, bd[...]) + mm_last(g2, bd2[...])
    put(out, picks, hidden, folded(adapter, mine[...]))


def up_kernel(*refs):
    up_part(*refs, range(CHIPS))


def up_back_kernel(*refs):
    up_back_part(*refs, range(CHIPS))


def turn_kernel(x_ref, mine, high, low, wu, wu2, au, au2, g_ref, wd, wd2, bd, bd2, out):
    n = 2 * CHIPS
    up_part(x_ref, mine, high, low, wu, wu2, au, au2, out, range(0, n, 2))
    up_back_part(g_ref, mine, wd, wd2, bd, bd2, out, range(1, n, 2))


def down_kernel(act_ref, wd, wd2, ad, mine, out):
    act = blocks(act_ref)
    width = wd.shape[1]
    picks = range(0, out.shape[0], 2), range(1, out.shape[0], 2)
    for pick, w in zip(picks, (wd, wd2)):
        for n, m in tiles(width):
            put(out, pick, n, mm(act, w[:, n:m]))
    adapter = folded(mm(act, ad[...]), mine[...])
    for pick in picks:
        put(out, pick, width, adapter)


def down_back_kernel(d_ref, wu, wu2, bu, x_ref, mine, out):
    both = blocks(d_ref)
    width, hidden = wu.shape
    d_s = both[:, :hidden]
    factors = jnp.sum(both[:, hidden:].astype(F32), axis=1, keepdims=True)
    picks = range(0, out.shape[0], 2), range(1, out.shape[0], 2)
    for j, w in enumerate((wu, wu2)):
        x = blocks(x_ref, j, 2)
        for n, m in tiles(width):
            put(out, picks[j], n, mm_last(d_s, w[n:m]) - x[:, n:m].astype(F32) * factors)
    adapter = folded(mm_last(d_s, bu[...]), mine[...])
    for pick in picks:
        put(out, pick, width, adapter)


def call(kernel, shape, *operands):
    macs = shape[0] * shape[1] * sum(o.size for o in operands if o.ndim == 2) // 2
    size = sum(o.size * o.dtype.itemsize for o in operands)
    return pl.pallas_call(
        kernel,
        out_shape=jax.ShapeDtypeStruct(shape, BF),
        in_specs=[pl.BlockSpec(memory_space=pltpu.VMEM)] * len(operands),
        out_specs=pl.BlockSpec(memory_space=pltpu.VMEM),
        compiler_params=pltpu.CompilerParams(vmem_limit_bytes=VMEM_LIMIT),
        cost_estimate=pl.CostEstimate(flops=2 * macs, bytes_accessed=size, transcendentals=0),
    )(*operands)


def load_kernel(*refs):
    n = len(refs) // 2
    sems = refs[-1]
    copies = [pltpu.make_async_copy(refs[i], refs[n + i], sems.at[i]) for i in range(n)]
    for copy in copies:
        copy.start()
    for copy in copies:
        copy.wait()


def resident(*arrays):
    n = len(arrays)
    return pl.pallas_call(
        load_kernel,
        out_shape=[pltpu.VMEM(a.shape, a.dtype) for a in arrays],
        in_specs=[pl.BlockSpec(memory_space=pltpu.MemorySpace.HBM)] * n,
        out_specs=[pl.BlockSpec(memory_space=pltpu.VMEM)] * n,
        scratch_shapes=[pltpu.SemaphoreType.DMA((n,))],
        compiler_params=pltpu.CompilerParams(vmem_limit_bytes=2**20),
    )(*arrays)


def to_all(value, n):
    return jnp.broadcast_to(value[None], (n,) + value.shape)


def total(parts):
    return jnp.sum(parts.astype(F32), axis=0)


def per_device(h_in, cotangent, w_up, w_down, a_up, b_up, a_down, b_down, job_ids, ranks):
    wu, wd, au, bu, ad, bd = (w_up[0], w_down[0], a_up[0], b_up[0], a_down[0], b_down[0])
    width, hidden = wu.shape
    lanes = au.shape[1]
    fold = lanes // 2
    replicas = lax.axis_size("dp")
    sections = lax.axis_size("pipe")
    section = lax.axis_index("pipe")
    block_at = lax.axis_index("dp") // CORES
    chip = lax.axis_index("tensor") // CORES
    core = lax.axis_index("tensor") % CORES
    block = MB * h_in.shape[1]
    rows = CHIPS * block

    wu2, au2, wd2, bd2 = [core_swap(w) for w in (wu, au, wd, bd)]

    col_job, scale = column_weights(ranks, lanes)
    jobs = jnp.broadcast_to(job_ids.T[:, :, None], job_ids.T.shape + (SEQ_LEN,))
    jobs = jobs.reshape(CORES, rows)
    jobs, jobs2 = [jnp.where(core == c, jobs[0], jobs[1])[:, None] for c in range(CORES)]
    lane = jnp.arange(fold, dtype=jnp.int32)[None, :]
    mine = (jobs == col_job[None, :]).astype(F32)
    mine2 = (jobs2 == col_job[None, :]).astype(F32)
    mask = mine * scale[None, :]
    free = RMAX * (1 - jobs % 2)
    high = (lane == free).astype(F32)
    low = (lane == free + 1).astype(F32)

    def cut(value, position):
        return lax.dynamic_slice_in_dim(value, position * block, block, 0)

    mask_share = cut(mask, chip)
    mask_own = cut(mask, block_at)
    both_share = cut(high + low, chip)

    ends = jnp.stack([v.reshape(block, width) for v in (h_in, cotangent)])
    masks = (mine, mine2, mask, high, low, mask_share, mask_own, both_share)
    place = lax.axis_index("dp").astype(jnp.uint32)
    flags = (place, core == 0, place % CORES == 0, section == 0, section == sections - 1)
    columns01 = (lane == 0, lane == 1)
    ready = lax.optimization_barrier((ends, masks, flags, columns01))
    ends, masks, (place, core0, half0, at_first, at_last), (lane0, lane1) = ready
    mine, mine2, mask, high, low, mask_share, mask_own, both_share = masks
    ends = dp_exchange(to_all(ends, replicas))
    ends, wu2, au2, wd2, bd2 = lax.optimization_barrier((ends, wu2, au2, wd2, bd2))
    kept = jnp.where(core0, ends[:CHIPS], ends[CHIPS:])
    sent = jnp.where(core0, ends[CHIPS:], ends[:CHIPS])
    got = core_swap(sent)
    x, g = [
        jnp.stack([kept[:, i], got[:, i]], axis=1).reshape(replicas, block, width)
        for i in range(2)
    ]
    zero = jnp.uint32(0)
    x_start, g_start = [
        lax.dynamic_slice(v, (place, zero, zero), (1, block, width))[0] for v in (x, g)
    ]
    x_own, g_own = x_start, g_start
    bd_own = jnp.where(half0, bd, bd2)
    au_own = jnp.where(half0, au, au2)
    weights = resident(wu, wu2, au, au2, wd, wd2, bd, bd2, bu, ad, bd_own, au_own)
    state = (x, g, x_start, x_own, g_start, g_own)
    state, weights = lax.optimization_barrier((state, weights))
    x, g, x_start, x_own, g_start, g_own = state
    wu, wu2, au, au2, wd, wd2, bd, bd2, bu, ad, bd_own, au_own = weights

    z_shape = (CHIPS, block, hidden + fold)
    dp_shape = (replicas, block, width + fold)
    ups, downs = (wu, wu2, au, au2), (wd, wd2, bd, bd2)

    def activate(summed):
        adapter = summed[:, hidden:]
        ss = jnp.sum(adapter * both_share, axis=1, keepdims=True)
        rs = lax.rsqrt(ss / D + EPS)
        qb = unfolded(adapter, mask_share)
        pre = summed[:, :hidden] + mm(qb, bu)
        u = rs * pre
        return rs, qb, pre, u, jax.nn.silu(u).astype(BF)

    for tick in range(sections - 1):
        act = activate(total(z_exchange(call(up_kernel, z_shape, x, mine, high, low, *ups))))[-1]
        act = z_exchange(to_all(act, CHIPS))
        y = total(dp_exchange(call(down_kernel, dp_shape, act, wd, wd2, ad, mine)))
        rb = unfolded(y[:, width:], mask_own)
        h = (x_own.astype(F32) + y[:, :width] + mm(rb, bd_own)).astype(BF)
        x_own = jnp.where(at_first, x_start, pipe_shift(h, 1))
        x = dp_exchange(to_all(x_own, replicas))

    turn_shape = (2 * CHIPS,) + z_shape[1:]
    summed = call(turn_kernel, turn_shape, x, mine, high, low, *ups, g, *downs)
    summed = total(z_exchange(summed.reshape((CHIPS, 2) + z_shape[1:])))
    rs, qb, pre, u, act = activate(summed[0])
    slope = silu_grad(u)
    d_sum = summed[1]

    def hidden_grads(d_sum):
        d_rb = unfolded(d_sum[:, hidden:], mask_share)
        d_u = (d_sum[:, :hidden] + mm_last(d_rb, ad)) * slope
        return d_rb, d_u, (d_u * rs).astype(BF)

    for tick in range(sections - 1):
        d_rb, d_u, d_sb = hidden_grads(d_sum)
        factor = (rs**3 / D) * jnp.sum(d_u * pre, axis=1, keepdims=True)
        top = lax.reduce_precision(factor, 8, 7)
        terms = jnp.where(lane0, top, jnp.where(lane1, factor - top, F32(0.0)))
        sent = jnp.concatenate([d_sb, terms.astype(BF)], axis=1)
        sent = z_exchange(to_all(sent, CHIPS))
        d = call(down_back_kernel, dp_shape, sent, wu, wu2, bu, x, mine)
        d = total(dp_exchange(d))
        d_qb = unfolded(d[:, width:], mask_own)
        d_x = g_own.astype(F32) + d[:, :width] + mm_last(d_qb, au_own)
        d_x = pipe_shift(d_x.astype(BF), -1)
        g_own = jnp.where(at_last, g_start, d_x)
        g = dp_exchange(to_all(g_own, replicas))
        d_sum = total(z_exchange(call(up_back_kernel, z_shape, g, mine, *downs)))

    d_rb, d_u, d_sb = hidden_grads(d_sum)
    group = lanes // CHIPS

    def by_chip(value):
        return jnp.swapaxes(value.reshape(block, CHIPS, group), 0, 1)

    sent = [to_all(d_sb, CHIPS), to_all(act, CHIPS), by_chip(qb), by_chip(d_rb)]
    first = z_exchange(jnp.concatenate(sent, axis=2)).reshape(rows, 2 * hidden + 2 * group)
    second = core_swap(first)
    d_q = folded(mm_last(first[:, :hidden], bu), mine)
    r = folded(mm(first[:, hidden : 2 * hidden], ad), mine)
    r = jnp.concatenate([r[:, RMAX:], r[:, :RMAX]], axis=1)
    sums = total(dp_exchange(to_all((d_q + r).astype(BF), replicas)))
    swapped = jnp.concatenate([sums[:, RMAX:], sums[:, :RMAX]], axis=1)
    d_qb, rb = unfolded(sums, mask), unfolded(swapped, mask)
    packed = [(v[:, :fold] + v[:, fold:]) for v in (d_qb, rb)]
    packed = core_swap(jnp.concatenate(packed, axis=1))
    d_qb2, rb2 = unfolded(packed[:, :fold], mine2), unfolded(packed[:, fold:], mine2)

    def columns(value):
        value = value.reshape(CHIPS, CORES, block, width)
        return value[:, 0].reshape(rows, width), core_swap(value[:, 1].reshape(rows, width))

    x, g, sums = lax.optimization_barrier((x, g, sums))
    (x, x2), (g, g2) = columns(x), columns(g)

    def outer(left, right, left2, right2):
        left = jnp.concatenate([left, left2], axis=0)
        return mm_first(left, jnp.concatenate([right, right2], axis=0))

    def parts(value):
        stops = [hidden, 2 * hidden, 2 * hidden + group]
        return jnp.split(value, stops, axis=1)

    (d_sb, act, qb, d_rb), (d_sb2, act2, qb2, d_rb2) = parts(first), parts(second)
    grad_au = outer(x, d_qb, x2, d_qb2)
    grad_bd = outer(rb, g, rb2, g2)
    grad_bu = outer(qb, d_sb, qb2, d_sb2)
    grad_ad = outer(act, d_rb, act2, d_rb2)
    piece = group // CORES
    grad_bu = lax.dynamic_slice_in_dim(grad_bu, core * piece, piece, 0)
    grad_ad = jnp.where(core0, grad_ad[:, :piece], grad_ad[:, piece:])
    return (grad_au[None], grad_bu[None], grad_ad[None], grad_bd[None])


def solution(mesh):
    in_specs = (
        P(None, "dp", "tensor"),
        P(None, "dp", "tensor"),
        P("pipe", "tensor", "dp"),
        P("pipe", "dp", "tensor"),
        P("pipe", "tensor", None),
        P("pipe", None, "dp"),
        P("pipe", "dp", None),
        P("pipe", None, "tensor"),
        P(),
        P(),
    )
    out_specs = (
        P("pipe", "tensor", None),
        P("pipe", "tensor", "dp"),
        P("pipe", "dp", "tensor"),
        P("pipe", None, "tensor"),
    )
    return jax.shard_map(
        per_device, mesh=mesh, in_specs=in_specs, out_specs=out_specs, check_vma=False
    )
```

```python
import jax
import jax.numpy as jnp
from jax import lax
from jax.experimental import pallas as pl
from jax.experimental.pallas import tpu as pltpu
from jax.sharding import PartitionSpec as P

D = 8192
RMAX = 64
JOBS = 4
MB = 2
SEQ_LEN = 12
CHIPS = 4
CORES = 2
VMEM_LIMIT = 12 * 2**20
LOAD_LIMITS = (48 * 2**20, 2**20)

EPS = 1e-05
ALPHA = 16.0

BF = jnp.bfloat16
F32 = jnp.float32
CHIP_STEPS = (0, 1, 3, 2)


def column_weights(ranks, lanes):
    column = jnp.arange(lanes, dtype=jnp.int32)
    col_job = column // RMAX
    picked = col_job[:, None] == jnp.arange(JOBS, dtype=jnp.int32)[None, :]
    rank_col = jnp.sum(jnp.where(picked, ranks[None, :], 0), axis=1)
    scale = jnp.where(
        column % RMAX < rank_col, ALPHA / rank_col.astype(jnp.float32), jnp.float32(0.0)
    )
    return (col_job, scale)


def silu_grad(u):
    sig = jax.nn.sigmoid(u)
    return sig * (1.0 + u * (1.0 - sig))


def mm(left, right):
    return jnp.dot(left, right, preferred_element_type=F32)


def mm_last(left, right):
    return lax.dot_general(left, right, (((1,), (1,)), ((), ())), preferred_element_type=F32)


def mm_first(left, right):
    return lax.dot_general(left, right, (((0,), (0,)), ((), ())), preferred_element_type=F32)


def core_swap(value):
    devices = lax.axis_size("tensor")
    return lax.ppermute(value, "tensor", [(i, i ^ 1) for i in range(devices)])


def chip_shift(value, step):
    n = lax.axis_size("tensor")
    return lax.ppermute(value, "tensor", [(i, (i + CORES * step) % n) for i in range(n)])


def z_sum(parts):
    got = [chip_shift(v, k) if k else v for v, k in zip(parts, CHIP_STEPS)]
    own, one, three, far = [v.astype(F32) for v in got]
    return far + one + three + own


def z_gather(value):
    return [chip_shift(value, -k) if k else value for k in CHIP_STEPS]


def dp_exchange(value):
    return lax.all_to_all(value, "dp", 0, 0)


def pipe_shift(value, step):
    n = lax.axis_size("pipe")
    return lax.ppermute(value, "pipe", [(i, (i + step) % n) for i in range(n)])


def blocks(refs):
    return jnp.concatenate([ref[...].astype(F32) for ref in refs], axis=0).astype(BF)


def halves(ref):
    return [[ref.at[i] for i in range(j, ref.shape[0], CORES)] for j in range(CORES)]


def folded(adapter, mine):
    kept = adapter * mine
    fold = kept.shape[1] // 2
    return kept[:, :fold] + kept[:, fold:]


def unfolded(value, mask):
    return (jnp.concatenate([value, value], axis=1) * mask).astype(BF)


def tiles(width, size=256):
    return [(n, min(n + size, width)) for n in range(0, width, size)]


def put(outs, start, value):
    rows = value.shape[0] // len(outs)
    stop = start + value.shape[1]
    for p, out in enumerate(outs):
        out[:, start:stop] = value[p * rows : (p + 1) * rows].astype(BF)


def up_part(x_ref, mine, high, low, wu, wu2, au, au2, outs):
    x, x2 = [blocks(half) for half in halves(x_ref)]
    hidden = wu.shape[1]
    for n, m in tiles(hidden):
        put(outs, n, mm(x, wu[:, n:m]) + mm(x2, wu2[:, n:m]))
    square = jnp.square(x.astype(F32)) + jnp.square(x2.astype(F32))
    ss = jnp.sum(square, axis=1, keepdims=True)
    top = ss.astype(BF).astype(F32)
    adapter = folded(mm(x, au[...]) + mm(x2, au2[...]), mine[...])
    put(outs, hidden, adapter + high[...] * top + low[...] * (ss - top))


def up_back_part(g_ref, mine, wd, wd2, bd, bd2, outs):
    g, g2 = [blocks(half) for half in halves(g_ref)]
    hidden = wd.shape[0]
    for n, m in tiles(hidden):
        put(outs, n, mm_last(g, wd[n:m]) + mm_last(g2, wd2[n:m]))
    adapter = mm_last(g, bd[...]) + mm_last(g2, bd2[...])
    put(outs, hidden, folded(adapter, mine[...]))


def up_kernel(*refs):
    up_part(*refs[:-CHIPS], refs[-CHIPS:])


def up_back_kernel(*refs):
    up_back_part(*refs[:-CHIPS], refs[-CHIPS:])


def turn_kernel(x_ref, mine, high, low, wu, wu2, au, au2, g_ref, wd, wd2, bd, bd2, *outs):
    up_part(x_ref, mine, high, low, wu, wu2, au, au2, [o.at[0] for o in outs])
    up_back_part(g_ref, mine, wd, wd2, bd, bd2, [o.at[1] for o in outs])


def down_kernel(*refs):
    mine, wd, wd2, ad, out = refs[CHIPS:]
    act = blocks(refs[:CHIPS])
    width = wd.shape[1]
    for outs, w in zip(halves(out), (wd, wd2)):
        for n, m in tiles(width):
            put(outs, n, mm(act, w[:, n:m]))
    adapter = folded(mm(act, ad[...]), mine[...])
    for outs in halves(out):
        put(outs, width, adapter)


def down_back_kernel(*refs):
    x_ref, mine, wu, wu2, bu, out = refs[CHIPS:]
    both = blocks(refs[:CHIPS])
    width, hidden = wu.shape
    d_s = both[:, :hidden]
    factors = jnp.sum(both[:, hidden:].astype(F32), axis=1, keepdims=True)
    for outs, half, w in zip(halves(out), halves(x_ref), (wu, wu2)):
        x = blocks(half)
        for n, m in tiles(width):
            put(outs, n, mm_last(d_s, w[n:m]) - x[:, n:m].astype(F32) * factors)
    adapter = folded(mm_last(d_s, bu[...]), mine[...])
    for outs in halves(out):
        put(outs, width, adapter)


def call(kernel, shapes, *operands):
    size = sum(o.size * o.dtype.itemsize for o in operands)
    macs = 96 * size // 2
    return pl.pallas_call(
        kernel,
        out_shape=[jax.ShapeDtypeStruct(shape, BF) for shape in shapes],
        in_specs=[pl.BlockSpec(memory_space=pltpu.VMEM)] * len(operands),
        out_specs=[pl.BlockSpec(memory_space=pltpu.VMEM)] * len(shapes),
        compiler_params=pltpu.CompilerParams(vmem_limit_bytes=VMEM_LIMIT),
        cost_estimate=pl.CostEstimate(flops=2 * macs, bytes_accessed=size, transcendentals=0),
    )(*operands)


def load_kernel(*refs):
    n = len(refs) // 2
    sems = refs[-1]
    copies = [pltpu.make_async_copy(refs[i], refs[n + i], sems.at[i]) for i in range(n)]
    for copy in copies:
        copy.start()
    for copy in copies:
        copy.wait()


def resident(limit, *arrays):
    n = len(arrays)
    return pl.pallas_call(
        load_kernel,
        out_shape=[pltpu.VMEM(a.shape, a.dtype) for a in arrays],
        in_specs=[pl.BlockSpec(memory_space=pltpu.MemorySpace.HBM)] * n,
        out_specs=[pl.BlockSpec(memory_space=pltpu.VMEM)] * n,
        scratch_shapes=[pltpu.SemaphoreType.DMA((n,))],
        compiler_params=pltpu.CompilerParams(vmem_limit_bytes=limit),
    )(*arrays)


def to_all(value, n):
    return jnp.broadcast_to(value[None], (n,) + value.shape)


def total(parts):
    return jnp.sum(parts.astype(F32), axis=0)


def per_device(h_in, cotangent, w_up, w_down, a_up, b_up, a_down, b_down, job_ids, ranks):
    wu, wd, au, bu, ad, bd = (w_up[0], w_down[0], a_up[0], b_up[0], a_down[0], b_down[0])
    width, hidden = wu.shape
    lanes = au.shape[1]
    fold = lanes // 2
    replicas = lax.axis_size("dp")
    sections = lax.axis_size("pipe")
    section = lax.axis_index("pipe")
    block_at = lax.axis_index("dp") // CORES
    core = lax.axis_index("tensor") % CORES
    block = MB * h_in.shape[1]
    rows = CHIPS * block

    wu2, au2, wd2, bd2 = [core_swap(w) for w in (wu, au, wd, bd)]

    col_job, scale = column_weights(ranks, lanes)
    jobs = jnp.broadcast_to(job_ids.T[:, :, None], job_ids.T.shape + (SEQ_LEN,))
    def turned(value, axis):
        value = jnp.concatenate([value, value], axis=axis)
        value = lax.dynamic_slice_in_dim(value, turn, CHIPS, axis)
        cuts = [lax.slice_in_dim(value, k, k + 1, axis=axis) for k in CHIP_STEPS]
        return jnp.concatenate(cuts, axis=axis)

    turn = (lax.axis_index("tensor") // CORES).astype(jnp.uint32)
    jobs = turned(jobs.reshape(CORES, CHIPS, block), 1).reshape(CORES, rows)
    jobs, jobs2 = [jnp.where(core == c, jobs[0], jobs[1])[:, None] for c in range(CORES)]
    lane = jnp.arange(fold, dtype=jnp.int32)[None, :]
    mine = (jobs == col_job[None, :]).astype(F32)
    mine2 = (jobs2 == col_job[None, :]).astype(F32)
    mask = mine * scale[None, :]
    free = RMAX * (1 - jobs % 2)
    high = (lane == free).astype(F32)
    low = (lane == free + 1).astype(F32)

    def cut(value, position):
        return lax.dynamic_slice_in_dim(value, position * block, block, 0)

    mask_share = mask[:block]
    mask_own = cut(mask, block_at)
    both_share = (high + low)[:block]

    ends = jnp.stack([v.reshape(block, width) for v in (h_in, cotangent)])
    ends = dp_exchange(to_all(ends, replicas))
    place = lax.axis_index("dp").astype(jnp.uint32)
    masks = (mine, mine2, mask, high, low, mask_share, mask_own, both_share)
    chip = turn.astype(jnp.int32)
    rows_here = ((jobs == chip).astype(BF), (jobs2 == chip).astype(BF))
    half0 = place % CORES == 0
    flags = (core == 0, half0, section == 0, section == sections - 1, chip % 2 == 0)
    columns01 = (lane == 0, lane == 1)
    owns = (jnp.where(half0, bd, bd2), jnp.where(half0, au, au2))
    aside = lax.optimization_barrier((ends, masks, flags, columns01, rows_here, owns, place, turn))
    ends, masks, flags, columns01, rows_here, owns, place, turn = aside
    core0 = flags[0]
    kept = jnp.where(core0, ends[:CHIPS], ends[CHIPS:])
    sent = jnp.where(core0, ends[CHIPS:], ends[:CHIPS])
    got = core_swap(sent)
    x, g = [
        turned(jnp.stack([kept[:, i], got[:, i]], axis=1), 0).reshape(replicas, block, width)
        for i in range(2)
    ]
    zero = jnp.uint32(0)
    x_start, g_start = [
        lax.dynamic_slice(v, (place, zero, zero), (1, block, width))[0] for v in (x, g)
    ]
    x_own, g_own = x_start, g_start
    ups = resident(LOAD_LIMITS[0], wu, wu2, au, au2)
    state = (x, g, x_start, x_own, g_start, g_own)
    ready = lax.optimization_barrier((state, ups, masks, flags, columns01, rows_here, owns))
    state, ups, masks, flags, (lane0, lane1), rows_here, owns = ready
    x, g, x_start, x_own, g_start, g_own = state
    mine, mine2, mask, high, low, mask_share, mask_own, both_share = masks
    core0, _, at_first, at_last, even = flags
    wu, wu2, au, au2 = ups

    z_shapes = [(block, hidden + fold)] * CHIPS
    dp_shape = (replicas, block, width + fold)
    parts = call(up_kernel, z_shapes, x, mine, high, low, *ups)
    others = lax.optimization_barrier((parts, wd, wd2, bd, bd2, bu, ad))
    parts, (wd, wd2, bd, bd2, bu, ad) = others[0], others[1:]
    held = resident(LOAD_LIMITS[1], wd, wd2, bd, bd2, bu, ad, *owns)
    wd, wd2, bd, bd2, bu, ad, bd_own, au_own = held
    downs = (wd, wd2, bd, bd2)

    def activate(summed):
        adapter = summed[:, hidden:]
        ss = jnp.sum(adapter * both_share, axis=1, keepdims=True)
        rs = lax.rsqrt(ss / D + EPS)
        qb = unfolded(adapter, mask_share)
        pre = summed[:, :hidden] + mm(qb, bu)
        u = rs * pre
        return rs, qb, pre, u, jax.nn.silu(u).astype(BF)

    for tick in range(sections - 1):
        if tick:
            parts = call(up_kernel, z_shapes, x, mine, high, low, *ups)
        act = activate(z_sum(parts))[-1]
        y = call(down_kernel, [dp_shape], *z_gather(act), mine, wd, wd2, ad)[0]
        y = total(dp_exchange(y))
        rb = unfolded(y[:, width:], mask_own)
        h = (x_own.astype(F32) + y[:, :width] + mm(rb, bd_own)).astype(BF)
        x_own = jnp.where(at_first, x_start, pipe_shift(h, 1))
        x = dp_exchange(to_all(x_own, replicas))

    shapes = [(2,) + shape for shape in z_shapes]
    summed = z_sum(call(turn_kernel, shapes, x, mine, high, low, *ups, g, *downs))
    rs, qb, pre, u, act = activate(summed[0])
    slope = silu_grad(u)
    d_sum = summed[1]

    def hidden_grads(d_sum):
        d_rb = unfolded(d_sum[:, hidden:], mask_share)
        d_u = (d_sum[:, :hidden] + mm_last(d_rb, ad)) * slope
        return d_rb, d_u, (d_u * rs).astype(BF)

    for tick in range(sections - 1):
        d_rb, d_u, d_sb = hidden_grads(d_sum)
        factor = (rs**3 / D) * jnp.sum(d_u * pre, axis=1, keepdims=True)
        top = lax.reduce_precision(factor, 8, 7)
        terms = jnp.where(lane0, top, jnp.where(lane1, factor - top, F32(0.0)))
        sent = jnp.concatenate([d_sb, terms.astype(BF)], axis=1)
        d = call(down_back_kernel, [dp_shape], *z_gather(sent), x, mine, wu, wu2, bu)[0]
        d = total(dp_exchange(d))
        d_qb = unfolded(d[:, width:], mask_own)
        d_x = g_own.astype(F32) + d[:, :width] + mm_last(d_qb, au_own)
        d_x = pipe_shift(d_x.astype(BF), -1)
        g_own = jnp.where(at_last, g_start, d_x)
        g = dp_exchange(to_all(g_own, replicas))
        d_sum = z_sum(call(up_back_kernel, z_shapes, g, mine, *downs))

    d_rb, d_u, d_sb = hidden_grads(d_sum)

    def packed(one, two):
        return jnp.concatenate([v[:, :fold] + v[:, fold:] for v in (one, two)], axis=1)

    def rows_of(values):
        value = jnp.concatenate(values, axis=0)
        return value, core_swap(value)

    x, g, d_sb = lax.optimization_barrier((x, g, d_sb))
    d_q = folded(mm_last(d_sb, bu), mine[:block])
    r = folded(mm(act, ad), mine[:block])
    sums = d_q + jnp.concatenate([r[:, RMAX:], r[:, :RMAX]], axis=1)
    sums = dp_exchange(to_all(sums.astype(BF), replicas))
    wide = z_gather(jnp.concatenate([d_sb, act, packed(qb, d_rb)], axis=1))
    sums, wide = lax.optimization_barrier((sums, wide))
    wide = rows_of(wide)
    sums = total(sums)
    swapped = jnp.concatenate([sums[:, RMAX:], sums[:, :RMAX]], axis=1)
    narrow = packed(unfolded(sums, mask_share), unfolded(swapped, mask_share))
    narrow = z_gather(narrow)

    def columns(value):
        value = value.reshape(CHIPS, CORES, block, width)
        return value[:, 0].reshape(rows, width), core_swap(value[:, 1].reshape(rows, width))

    xs, gs = columns(x), columns(g)
    piece = lanes // (CHIPS * CORES)

    def own_lanes(value, here):
        cuts = [value[:, i : i + piece] for i in range(0, fold, piece)]
        cuts = [jnp.where(core0, *pair) for pair in (cuts[:2], cuts[2:])]
        return jnp.where(even, *cuts) * here

    def outer(left, right):
        return mm_first(*[jnp.concatenate(side, axis=0) for side in (left, right)])

    qbs = [own_lanes(v[:, 2 * hidden : 2 * hidden + fold], h) for v, h in zip(wide, rows_here)]
    d_rbs = [own_lanes(v[:, 2 * hidden + fold :], h) for v, h in zip(wide, rows_here)]
    grad_bu = outer(qbs, [v[:, :hidden] for v in wide])
    grad_ad = outer([v[:, hidden : 2 * hidden] for v in wide], d_rbs)
    narrow, grad_bu, grad_ad = lax.optimization_barrier((narrow, grad_bu, grad_ad))
    both = list(zip(rows_of(narrow), (mine, mine2)))
    grad_au = outer(xs, [unfolded(v[:, :fold], m) for v, m in both])
    grad_bd = outer([unfolded(v[:, fold:], m) for v, m in both], gs)
    return (grad_au[None], grad_bu[None], grad_ad[None], grad_bd[None])


def solution(mesh):
    in_specs = (
        P(None, "dp", "tensor"),
        P(None, "dp", "tensor"),
        P("pipe", "tensor", "dp"),
        P("pipe", "dp", "tensor"),
        P("pipe", "tensor", None),
        P("pipe", None, "dp"),
        P("pipe", "dp", None),
        P("pipe", None, "tensor"),
        P(),
        P(),
    )
    out_specs = (
        P("pipe", "tensor", None),
        P("pipe", "tensor", "dp"),
        P("pipe", "dp", "tensor"),
        P("pipe", None, "tensor"),
    )
    return jax.shard_map(
        per_device, mesh=mesh, in_specs=in_specs, out_specs=out_specs, check_vma=False
    )
```

```python
import jax
import jax.numpy as jnp
from jax import lax
from jax.experimental import pallas as pl
from jax.experimental.pallas import tpu as pltpu
from jax.sharding import PartitionSpec as P

D = 8192
RMAX = 64
JOBS = 4
MB = 2
SEQ_LEN = 12
CHIPS = 4
CORES = 2
VMEM_LIMIT = 12 * 2**20
LOAD_LIMITS = (48 * 2**20, 2**20)

EPS = 1e-05
ALPHA = 16.0

BF = jnp.bfloat16
F32 = jnp.float32
CHIP_STEPS = (0, 1, 3, 2)


def column_weights(ranks, lanes):
    column = jnp.arange(lanes, dtype=jnp.int32)
    col_job = column // RMAX
    picked = col_job[:, None] == jnp.arange(JOBS, dtype=jnp.int32)[None, :]
    rank_col = jnp.sum(jnp.where(picked, ranks[None, :], 0), axis=1)
    scale = jnp.where(
        column % RMAX < rank_col, ALPHA / rank_col.astype(jnp.float32), jnp.float32(0.0)
    )
    return (col_job, scale)


def silu_grad(u):
    sig = jax.nn.sigmoid(u)
    return sig * (1.0 + u * (1.0 - sig))


def mm(left, right):
    return jnp.dot(left, right, preferred_element_type=F32)


def mm_last(left, right):
    return lax.dot_general(left, right, (((1,), (1,)), ((), ())), preferred_element_type=F32)


def mm_first(left, right):
    return lax.dot_general(left, right, (((0,), (0,)), ((), ())), preferred_element_type=F32)


def core_swap(value):
    devices = lax.axis_size("tensor")
    return lax.ppermute(value, "tensor", [(i, i ^ 1) for i in range(devices)])


def chip_shift(value, step):
    n = lax.axis_size("tensor")
    return lax.ppermute(value, "tensor", [(i, (i + CORES * step) % n) for i in range(n)])


def z_sum(parts):
    got = [chip_shift(v, k) if k else v for v, k in zip(parts, CHIP_STEPS)]
    own, one, three, far = [v.astype(F32) for v in got]
    return far + one + three + own


def z_gather(value):
    return [chip_shift(value, -k) if k else value for k in CHIP_STEPS]


def dp_exchange(value):
    return lax.all_to_all(value, "dp", 0, 0)


def pipe_shift(value, step):
    n = lax.axis_size("pipe")
    return lax.ppermute(value, "pipe", [(i, (i + step) % n) for i in range(n)])


def blocks(refs):
    return jnp.concatenate([ref[...].astype(F32) for ref in refs], axis=0).astype(BF)


def halves(ref):
    return [[ref.at[i] for i in range(j, ref.shape[0], CORES)] for j in range(CORES)]


def folded(adapter, mine):
    kept = adapter * mine
    fold = kept.shape[1] // 2
    return kept[:, :fold] + kept[:, fold:]


def unfolded(value, mask):
    return (jnp.concatenate([value, value], axis=1) * mask).astype(BF)


def tiles(width, size=256):
    return [(n, min(n + size, width)) for n in range(0, width, size)]


def put(outs, start, value):
    rows = value.shape[0] // len(outs)
    stop = start + value.shape[1]
    for p, out in enumerate(outs):
        out[:, start:stop] = value[p * rows : (p + 1) * rows].astype(BF)


def up_part(x_ref, mine, high, low, wu, wu2, au, au2, outs):
    x, x2 = [blocks(half) for half in halves(x_ref)]
    hidden = wu.shape[1]
    for n, m in tiles(hidden):
        put(outs, n, mm(x, wu[:, n:m]) + mm(x2, wu2[:, n:m]))
    square = jnp.square(x.astype(F32)) + jnp.square(x2.astype(F32))
    ss = jnp.sum(square, axis=1, keepdims=True)
    top = ss.astype(BF).astype(F32)
    adapter = folded(mm(x, au[...]) + mm(x2, au2[...]), mine[...])
    put(outs, hidden, adapter + high[...] * top + low[...] * (ss - top))


def up_back_part(g_ref, mine, wd, wd2, bd, bd2, outs):
    g, g2 = [blocks(half) for half in halves(g_ref)]
    hidden = wd.shape[1]
    for n, m in tiles(hidden):
        put(outs, n, mm(g, wd[:, n:m]) + mm(g2, wd2[:, n:m]))
    adapter = mm_last(g, bd[...]) + mm_last(g2, bd2[...])
    put(outs, hidden, folded(adapter, mine[...]))


def up_kernel(*refs):
    up_part(*refs[:-CHIPS], refs[-CHIPS:])


def up_back_kernel(*refs):
    up_back_part(*refs[:-CHIPS], refs[-CHIPS:])


def turn_kernel(x_ref, mine, high, low, wu, wu2, au, au2, g_ref, wd, wd2, bd, bd2, *outs):
    up_part(x_ref, mine, high, low, wu, wu2, au, au2, [o.at[0] for o in outs])
    up_back_part(g_ref, mine, wd, wd2, bd, bd2, [o.at[1] for o in outs])


def down_kernel(*refs):
    mine, wd, wd2, ad, out = refs[CHIPS:]
    act = blocks(refs[:CHIPS])
    width = wd.shape[1]
    for outs, w in zip(halves(out), (wd, wd2)):
        for n, m in tiles(width):
            put(outs, n, mm(act, w[:, n:m]))
    adapter = folded(mm(act, ad[...]), mine[...])
    for outs in halves(out):
        put(outs, width, adapter)


def down_back_kernel(*refs):
    x_ref, mine, wu, wu2, bu, out = refs[CHIPS:]
    both = blocks(refs[:CHIPS])
    hidden, width = wu.shape
    d_s = both[:, :hidden]
    factors = jnp.sum(both[:, hidden:].astype(F32), axis=1, keepdims=True)
    for outs, half, w in zip(halves(out), halves(x_ref), (wu, wu2)):
        x = blocks(half)
        for n, m in tiles(width):
            put(outs, n, mm(d_s, w[:, n:m]) - x[:, n:m].astype(F32) * factors)
    adapter = folded(mm_last(d_s, bu[...]), mine[...])
    for outs in halves(out):
        put(outs, width, adapter)


def call(kernel, shapes, *operands):
    size = sum(o.size * o.dtype.itemsize for o in operands)
    macs = 96 * size // 2
    return pl.pallas_call(
        kernel,
        out_shape=[jax.ShapeDtypeStruct(shape, BF) for shape in shapes],
        in_specs=[pl.BlockSpec(memory_space=pltpu.VMEM)] * len(operands),
        out_specs=[pl.BlockSpec(memory_space=pltpu.VMEM)] * len(shapes),
        compiler_params=pltpu.CompilerParams(vmem_limit_bytes=VMEM_LIMIT),
        cost_estimate=pl.CostEstimate(flops=2 * macs, bytes_accessed=size, transcendentals=0),
    )(*operands)


def load_kernel(*refs):
    n = len(refs) // 2
    sems = refs[-1]
    copies = [pltpu.make_async_copy(refs[i], refs[n + i], sems.at[i]) for i in range(n)]
    for copy in copies:
        copy.start()
    for copy in copies:
        copy.wait()


def resident(limit, *arrays):
    n = len(arrays)
    return pl.pallas_call(
        load_kernel,
        out_shape=[pltpu.VMEM(a.shape, a.dtype) for a in arrays],
        in_specs=[pl.BlockSpec(memory_space=pltpu.MemorySpace.HBM)] * n,
        out_specs=[pl.BlockSpec(memory_space=pltpu.VMEM)] * n,
        scratch_shapes=[pltpu.SemaphoreType.DMA((n,))],
        compiler_params=pltpu.CompilerParams(vmem_limit_bytes=limit),
    )(*arrays)


def transpose_kernel(a, b, at, bt):
    for source, out in ((a, at), (b, bt)):
        for n, m in tiles(source.shape[0]):
            out[:, n:m] = source[n:m].T


def transposed(a, b):
    return pl.pallas_call(
        transpose_kernel,
        out_shape=[pltpu.VMEM(v.shape[::-1], v.dtype) for v in (a, b)],
        in_specs=[pl.BlockSpec(memory_space=pltpu.VMEM)] * 2,
        out_specs=[pl.BlockSpec(memory_space=pltpu.VMEM)] * 2,
        compiler_params=pltpu.CompilerParams(vmem_limit_bytes=VMEM_LIMIT),
    )(a, b)


def to_all(value, n):
    return jnp.broadcast_to(value[None], (n,) + value.shape)


def total(parts):
    return jnp.sum(parts.astype(F32), axis=0)


def per_device(h_in, cotangent, w_up, w_down, a_up, b_up, a_down, b_down, job_ids, ranks):
    wu, wd, au, bu, ad, bd = (w_up[0], w_down[0], a_up[0], b_up[0], a_down[0], b_down[0])
    width, hidden = wu.shape
    lanes = au.shape[1]
    fold = lanes // 2
    replicas = lax.axis_size("dp")
    sections = lax.axis_size("pipe")
    section = lax.axis_index("pipe")
    block_at = lax.axis_index("dp") // CORES
    core = lax.axis_index("tensor") % CORES
    block = MB * h_in.shape[1]
    rows = CHIPS * block

    wu2, au2, wd2, bd2 = [core_swap(w) for w in (wu, au, wd, bd)]

    col_job, scale = column_weights(ranks, lanes)
    jobs = jnp.broadcast_to(job_ids.T[:, :, None], job_ids.T.shape + (SEQ_LEN,))
    def turned(value, axis):
        value = jnp.concatenate([value, value], axis=axis)
        value = lax.dynamic_slice_in_dim(value, turn, CHIPS, axis)
        cuts = [lax.slice_in_dim(value, k, k + 1, axis=axis) for k in CHIP_STEPS]
        return jnp.concatenate(cuts, axis=axis)

    turn = (lax.axis_index("tensor") // CORES).astype(jnp.uint32)
    jobs = turned(jobs.reshape(CORES, CHIPS, block), 1).reshape(CORES, rows)
    jobs, jobs2 = [jnp.where(core == c, jobs[0], jobs[1])[:, None] for c in range(CORES)]
    lane = jnp.arange(fold, dtype=jnp.int32)[None, :]
    mine = (jobs == col_job[None, :]).astype(F32)
    mine2 = (jobs2 == col_job[None, :]).astype(F32)
    mask = mine * scale[None, :]
    free = RMAX * (1 - jobs % 2)
    high = (lane == free).astype(F32)
    low = (lane == free + 1).astype(F32)

    def cut(value, position):
        return lax.dynamic_slice_in_dim(value, position * block, block, 0)

    mask_share = mask[:block]
    mask_own = cut(mask, block_at)
    both_share = (high + low)[:block]

    ends = jnp.stack([v.reshape(block, width) for v in (h_in, cotangent)])
    ends = dp_exchange(to_all(ends, replicas))
    place = lax.axis_index("dp").astype(jnp.uint32)
    masks = (mine, mine2, mask, high, low, mask_share, mask_own, both_share)
    chip = turn.astype(jnp.int32)
    rows_here = ((jobs == chip).astype(BF), (jobs2 == chip).astype(BF))
    half0 = place % CORES == 0
    flags = (core == 0, half0, section == 0, section == sections - 1, chip % 2 == 0)
    columns01 = (lane == 0, lane == 1)
    owns = (jnp.where(half0, bd, bd2), jnp.where(half0, au, au2))
    aside = lax.optimization_barrier((ends, masks, flags, columns01, rows_here, owns, place, turn))
    ends, masks, flags, columns01, rows_here, owns, place, turn = aside
    core0 = flags[0]
    kept = jnp.where(core0, ends[:CHIPS], ends[CHIPS:])
    sent = jnp.where(core0, ends[CHIPS:], ends[:CHIPS])
    got = core_swap(sent)
    x, g = [
        turned(jnp.stack([kept[:, i], got[:, i]], axis=1), 0).reshape(replicas, block, width)
        for i in range(2)
    ]
    zero = jnp.uint32(0)
    x_start, g_start = [
        lax.dynamic_slice(v, (place, zero, zero), (1, block, width))[0] for v in (x, g)
    ]
    x_own, g_own = x_start, g_start
    ups = resident(LOAD_LIMITS[0], wu, wu2, au, au2)
    state = (x, g, x_start, x_own, g_start, g_own)
    ready = lax.optimization_barrier((state, ups, masks, flags, columns01, rows_here, owns))
    state, ups, masks, flags, (lane0, lane1), rows_here, owns = ready
    x, g, x_start, x_own, g_start, g_own = state
    mine, mine2, mask, high, low, mask_share, mask_own, both_share = masks
    core0, _, at_first, at_last, even = flags
    wu, wu2, au, au2 = ups

    z_shapes = [(block, hidden + fold)] * CHIPS
    dp_shape = (replicas, block, width + fold)
    parts = call(up_kernel, z_shapes, x, mine, high, low, *ups)
    others = lax.optimization_barrier((parts, wd, wd2, bd, bd2, bu, ad))
    parts, (wd, wd2, bd, bd2, bu, ad) = others[0], others[1:]
    held = resident(LOAD_LIMITS[1], wd, wd2, bd, bd2, bu, ad, *owns)
    wd, wd2, bd, bd2, bu, ad, bd_own, au_own = held

    def activate(summed):
        adapter = summed[:, hidden:]
        ss = jnp.sum(adapter * both_share, axis=1, keepdims=True)
        rs = lax.rsqrt(ss / D + EPS)
        qb = unfolded(adapter, mask_share)
        pre = summed[:, :hidden] + mm(qb, bu)
        u = rs * pre
        return rs, qb, pre, u, jax.nn.silu(u).astype(BF)

    turned_weights = {}
    for tick in range(sections - 1):
        if tick:
            parts = call(up_kernel, z_shapes, x, mine, high, low, *ups)
        act = activate(z_sum(parts))[-1]
        if not tick:
            acts = z_gather(act)
        else:
            act, *pair = lax.optimization_barrier((act, *((wu, wu2) if tick == 1 else (wd, wd2))))
            acts = z_gather(act)
            turned_weights[tick] = transposed(*pair)
            acts, turned_weights[tick] = lax.optimization_barrier((acts, turned_weights[tick]))
        y = call(down_kernel, [dp_shape], *acts, mine, wd, wd2, ad)[0]
        y = total(dp_exchange(y))
        rb = unfolded(y[:, width:], mask_own)
        h = (x_own.astype(F32) + y[:, :width] + mm(rb, bd_own)).astype(BF)
        x_own = jnp.where(at_first, x_start, pipe_shift(h, 1))
        x = dp_exchange(to_all(x_own, replicas))

    (wu_t, wu2_t), (wd_t, wd2_t) = turned_weights[1], turned_weights[2]
    downs = (wd_t, wd2_t, bd, bd2)
    shapes = [(2,) + shape for shape in z_shapes]
    summed = z_sum(call(turn_kernel, shapes, x, mine, high, low, *ups, g, *downs))
    rs, qb, pre, u, act = activate(summed[0])
    slope = silu_grad(u)
    d_sum = summed[1]

    def hidden_grads(d_sum):
        d_rb = unfolded(d_sum[:, hidden:], mask_share)
        d_u = (d_sum[:, :hidden] + mm_last(d_rb, ad)) * slope
        return d_rb, d_u, (d_u * rs).astype(BF)

    for tick in range(sections - 1):
        d_rb, d_u, d_sb = hidden_grads(d_sum)
        factor = (rs**3 / D) * jnp.sum(d_u * pre, axis=1, keepdims=True)
        top = lax.reduce_precision(factor, 8, 7)
        terms = jnp.where(lane0, top, jnp.where(lane1, factor - top, F32(0.0)))
        sent = jnp.concatenate([d_sb, terms.astype(BF)], axis=1)
        d = call(down_back_kernel, [dp_shape], *z_gather(sent), x, mine, wu_t, wu2_t, bu)[0]
        d = total(dp_exchange(d))
        d_qb = unfolded(d[:, width:], mask_own)
        d_x = g_own.astype(F32) + d[:, :width] + mm_last(d_qb, au_own)
        d_x = pipe_shift(d_x.astype(BF), -1)
        g_own = jnp.where(at_last, g_start, d_x)
        g = dp_exchange(to_all(g_own, replicas))
        d_sum = z_sum(call(up_back_kernel, z_shapes, g, mine, *downs))

    d_rb, d_u, d_sb = hidden_grads(d_sum)

    def packed(one, two):
        return jnp.concatenate([v[:, :fold] + v[:, fold:] for v in (one, two)], axis=1)

    def rows_of(values):
        value = jnp.concatenate(values, axis=0)
        return value, core_swap(value)

    x, g, d_sb = lax.optimization_barrier((x, g, d_sb))
    d_q = folded(mm_last(d_sb, bu), mine[:block])
    r = folded(mm(act, ad), mine[:block])
    sums = d_q + jnp.concatenate([r[:, RMAX:], r[:, :RMAX]], axis=1)
    sums = dp_exchange(to_all(sums.astype(BF), replicas))
    wide = z_gather(jnp.concatenate([d_sb, act, packed(qb, d_rb)], axis=1))
    sums, wide = lax.optimization_barrier((sums, wide))
    wide = rows_of(wide)
    sums = total(sums)
    swapped = jnp.concatenate([sums[:, RMAX:], sums[:, :RMAX]], axis=1)
    narrow = packed(unfolded(sums, mask_share), unfolded(swapped, mask_share))
    narrow = z_gather(narrow)

    def columns(value):
        value = value.reshape(CHIPS, CORES, block, width)
        return value[:, 0].reshape(rows, width), core_swap(value[:, 1].reshape(rows, width))

    xs, gs = columns(x), columns(g)
    piece = lanes // (CHIPS * CORES)

    def own_lanes(value, here):
        cuts = [value[:, i : i + piece] for i in range(0, fold, piece)]
        cuts = [jnp.where(core0, *pair) for pair in (cuts[:2], cuts[2:])]
        return jnp.where(even, *cuts) * here

    def outer(left, right):
        return mm_first(*[jnp.concatenate(side, axis=0) for side in (left, right)])

    qbs = [own_lanes(v[:, 2 * hidden : 2 * hidden + fold], h) for v, h in zip(wide, rows_here)]
    d_rbs = [own_lanes(v[:, 2 * hidden + fold :], h) for v, h in zip(wide, rows_here)]
    grad_bu = outer(qbs, [v[:, :hidden] for v in wide])
    grad_ad = outer([v[:, hidden : 2 * hidden] for v in wide], d_rbs)
    narrow, grad_bu, grad_ad = lax.optimization_barrier((narrow, grad_bu, grad_ad))
    both = list(zip(rows_of(narrow), (mine, mine2)))
    grad_au = outer(xs, [unfolded(v[:, :fold], m) for v, m in both])
    grad_bd = outer([unfolded(v[:, fold:], m) for v, m in both], gs)
    return (grad_au[None], grad_bu[None], grad_ad[None], grad_bd[None])


def solution(mesh):
    in_specs = (
        P(None, "dp", "tensor"),
        P(None, "dp", "tensor"),
        P("pipe", "tensor", "dp"),
        P("pipe", "dp", "tensor"),
        P("pipe", "tensor", None),
        P("pipe", None, "dp"),
        P("pipe", "dp", None),
        P("pipe", None, "tensor"),
        P(),
        P(),
    )
    out_specs = (
        P("pipe", "tensor", None),
        P("pipe", "tensor", "dp"),
        P("pipe", "dp", "tensor"),
        P("pipe", None, "tensor"),
    )
    return jax.shard_map(
        per_device, mesh=mesh, in_specs=in_specs, out_specs=out_specs, check_vma=False
    )
```

```python
import jax
import jax.numpy as jnp
from jax import lax
from jax.experimental import pallas as pl
from jax.experimental.pallas import tpu as pltpu
from jax.sharding import PartitionSpec as P

D = 8192
RMAX = 64
JOBS = 4
MB = 2
SEQ_LEN = 12
CHIPS = 4
CORES = 2
VMEM_LIMIT = 12 * 2**20
LOAD_LIMITS = (48 * 2**20, 2**20)

EPS = 1e-05
ALPHA = 16.0

BF = jnp.bfloat16
F32 = jnp.float32
CHIP_STEPS = (0, 1, 3, 2)


def column_weights(ranks, lanes):
    column = jnp.arange(lanes, dtype=jnp.int32)
    col_job = column // RMAX
    picked = col_job[:, None] == jnp.arange(JOBS, dtype=jnp.int32)[None, :]
    rank_col = jnp.sum(jnp.where(picked, ranks[None, :], 0), axis=1)
    scale = jnp.where(
        column % RMAX < rank_col, ALPHA / rank_col.astype(jnp.float32), jnp.float32(0.0)
    )
    return (col_job, scale)


def silu_grad(u):
    sig = jax.nn.sigmoid(u)
    return sig * (1.0 + u * (1.0 - sig))


def mm(left, right):
    return jnp.dot(left, right, preferred_element_type=F32)


def mm_last(left, right):
    return lax.dot_general(left, right, (((1,), (1,)), ((), ())), preferred_element_type=F32)


def mm_first(left, right):
    return lax.dot_general(left, right, (((0,), (0,)), ((), ())), preferred_element_type=F32)


def core_swap(value):
    devices = lax.axis_size("tensor")
    return lax.ppermute(value, "tensor", [(i, i ^ 1) for i in range(devices)])


def chip_shift(value, step):
    n = lax.axis_size("tensor")
    return lax.ppermute(value, "tensor", [(i, (i + CORES * step) % n) for i in range(n)])


def z_sum(parts):
    got = [chip_shift(v, k) if k else v for v, k in zip(parts, CHIP_STEPS)]
    own, one, three, far = [v.astype(F32) for v in got]
    return far + one + three + own


def z_gather(value):
    return [chip_shift(value, -k) if k else value for k in CHIP_STEPS]


def dp_exchange(value):
    return lax.all_to_all(value, "dp", 0, 0)


def pipe_shift(value, step):
    n = lax.axis_size("pipe")
    return lax.ppermute(value, "pipe", [(i, (i + step) % n) for i in range(n)])


def blocks(refs):
    return jnp.concatenate([ref[...].astype(F32) for ref in refs], axis=0).astype(BF)


def halves(ref):
    return [[ref.at[i] for i in range(j, ref.shape[0], CORES)] for j in range(CORES)]


def folded(adapter, mine):
    kept = adapter * mine
    fold = kept.shape[1] // 2
    return kept[:, :fold] + kept[:, fold:]


def unfolded(value, mask):
    return (jnp.concatenate([value, value], axis=1) * mask).astype(BF)


def tiles(width, size=256):
    return [(n, min(n + size, width)) for n in range(0, width, size)]


def put(outs, start, value):
    rows = value.shape[0] // len(outs)
    stop = start + value.shape[1]
    for p, out in enumerate(outs):
        out[:, start:stop] = value[p * rows : (p + 1) * rows].astype(BF)


def up_part(x_ref, mine, high, low, wu, wu2, au, au2, outs):
    x, x2 = [blocks(half) for half in halves(x_ref)]
    hidden = wu.shape[1]
    for n, m in tiles(hidden):
        put(outs, n, mm(x, wu[:, n:m]) + mm(x2, wu2[:, n:m]))
    square = jnp.square(x.astype(F32)) + jnp.square(x2.astype(F32))
    ss = jnp.sum(square, axis=1, keepdims=True)
    top = ss.astype(BF).astype(F32)
    adapter = folded(mm(x, au[...]) + mm(x2, au2[...]), mine[...])
    put(outs, hidden, adapter + high[...] * top + low[...] * (ss - top))


def up_back_part(g_ref, mine, wd, wd2, bd, bd2, outs):
    g, g2 = [blocks(half) for half in halves(g_ref)]
    hidden = wd.shape[1]
    for n, m in tiles(hidden):
        put(outs, n, mm(g, wd[:, n:m]) + mm(g2, wd2[:, n:m]))
    adapter = mm_last(g, bd[...]) + mm_last(g2, bd2[...])
    put(outs, hidden, folded(adapter, mine[...]))


def up_kernel(*refs):
    up_part(*refs[:-CHIPS], refs[-CHIPS:])


def up_back_kernel(*refs):
    up_back_part(*refs[:-CHIPS], refs[-CHIPS:])


def turn_kernel(x_ref, mine, high, low, wu, wu2, au, au2, g_ref, wd, wd2, bd, bd2, *outs):
    up_part(x_ref, mine, high, low, wu, wu2, au, au2, [o.at[0] for o in outs])
    up_back_part(g_ref, mine, wd, wd2, bd, bd2, [o.at[1] for o in outs])


def down_kernel(*refs):
    mine, wd, wd2, ad, out = refs[CHIPS:]
    act = blocks(refs[:CHIPS])
    width = wd.shape[1]
    for outs, w in zip(halves(out), (wd, wd2)):
        for n, m in tiles(width):
            put(outs, n, mm(act, w[:, n:m]))
    adapter = folded(mm(act, ad[...]), mine[...])
    for outs in halves(out):
        put(outs, width, adapter)


def down_back_kernel(*refs):
    x_ref, mine, wu, wu2, bu, out = refs[CHIPS:]
    both = blocks(refs[:CHIPS])
    hidden, width = wu.shape
    d_s = both[:, :hidden]
    factors = jnp.sum(both[:, hidden:].astype(F32), axis=1, keepdims=True)
    for outs, half, w in zip(halves(out), halves(x_ref), (wu, wu2)):
        x = blocks(half)
        for n, m in tiles(width):
            put(outs, n, mm(d_s, w[:, n:m]) - x[:, n:m].astype(F32) * factors)
    adapter = folded(mm_last(d_s, bu[...]), mine[...])
    for outs in halves(out):
        put(outs, width, adapter)


def call(kernel, shapes, *operands):
    size = sum(o.size * o.dtype.itemsize for o in operands)
    macs = 96 * size // 2
    return pl.pallas_call(
        kernel,
        out_shape=[jax.ShapeDtypeStruct(shape, BF) for shape in shapes],
        in_specs=[pl.BlockSpec(memory_space=pltpu.VMEM)] * len(operands),
        out_specs=[pl.BlockSpec(memory_space=pltpu.VMEM)] * len(shapes),
        compiler_params=pltpu.CompilerParams(vmem_limit_bytes=VMEM_LIMIT),
        cost_estimate=pl.CostEstimate(flops=2 * macs, bytes_accessed=size, transcendentals=0),
    )(*operands)


def load_kernel(*refs):
    n = len(refs) // 2
    sems = refs[-1]
    copies = [pltpu.make_async_copy(refs[i], refs[n + i], sems.at[i]) for i in range(n)]
    for copy in copies:
        copy.start()
    for copy in copies:
        copy.wait()


def resident(limit, *arrays):
    n = len(arrays)
    return pl.pallas_call(
        load_kernel,
        out_shape=[pltpu.VMEM(a.shape, a.dtype) for a in arrays],
        in_specs=[pl.BlockSpec(memory_space=pltpu.MemorySpace.HBM)] * n,
        out_specs=[pl.BlockSpec(memory_space=pltpu.VMEM)] * n,
        scratch_shapes=[pltpu.SemaphoreType.DMA((n,))],
        compiler_params=pltpu.CompilerParams(vmem_limit_bytes=limit),
    )(*arrays)


def transpose_kernel(a, b, at, bt):
    for source, out in ((a, at), (b, bt)):
        for n, m in tiles(source.shape[0]):
            out[:, n:m] = source[n:m].T


def transposed(a, b):
    return pl.pallas_call(
        transpose_kernel,
        out_shape=[pltpu.VMEM(v.shape[::-1], v.dtype) for v in (a, b)],
        in_specs=[pl.BlockSpec(memory_space=pltpu.VMEM)] * 2,
        out_specs=[pl.BlockSpec(memory_space=pltpu.VMEM)] * 2,
        compiler_params=pltpu.CompilerParams(vmem_limit_bytes=VMEM_LIMIT),
    )(a, b)


def to_all(value, n):
    return jnp.broadcast_to(value[None], (n,) + value.shape)


def total(parts):
    return jnp.sum(parts.astype(F32), axis=0)


def per_device(h_in, cotangent, w_up, w_down, a_up, b_up, a_down, b_down, job_ids, ranks):
    wu, wd, au, bu, ad, bd = (w_up[0], w_down[0], a_up[0], b_up[0], a_down[0], b_down[0])
    width, hidden = wu.shape
    lanes = au.shape[1]
    fold = lanes // 2
    replicas = lax.axis_size("dp")
    sections = lax.axis_size("pipe")
    section = lax.axis_index("pipe")
    block_at = lax.axis_index("dp") // CORES
    core = lax.axis_index("tensor") % CORES
    block = MB * h_in.shape[1]
    rows = CHIPS * block

    wu2, au2, wd2, bd2 = [core_swap(w) for w in (wu, au, wd, bd)]

    col_job, scale = column_weights(ranks, lanes)
    jobs = jnp.broadcast_to(job_ids.T[:, :, None], job_ids.T.shape + (SEQ_LEN,))
    def turned(value, axis):
        value = jnp.concatenate([value, value], axis=axis)
        value = lax.dynamic_slice_in_dim(value, turn, CHIPS, axis)
        cuts = [lax.slice_in_dim(value, k, k + 1, axis=axis) for k in CHIP_STEPS]
        return jnp.concatenate(cuts, axis=axis)

    turn = (lax.axis_index("tensor") // CORES).astype(jnp.uint32)
    jobs = turned(jobs.reshape(CORES, CHIPS, block), 1).reshape(CORES, rows)
    jobs, jobs2 = [jnp.where(core == c, jobs[0], jobs[1])[:, None] for c in range(CORES)]
    lane = jnp.arange(fold, dtype=jnp.int32)[None, :]
    mine = (jobs == col_job[None, :]).astype(F32)
    mine2 = (jobs2 == col_job[None, :]).astype(F32)
    mask = mine * scale[None, :]
    free = RMAX * (1 - jobs % 2)
    high = (lane == free).astype(F32)
    low = (lane == free + 1).astype(F32)

    def cut(value, position):
        return lax.dynamic_slice_in_dim(value, position * block, block, 0)

    mask_share = mask[:block]
    mask_own = cut(mask, block_at)
    both_share = (high + low)[:block]

    ends = jnp.stack([v.reshape(block, width) for v in (h_in, cotangent)])
    ends = dp_exchange(to_all(ends, replicas))
    place = lax.axis_index("dp").astype(jnp.uint32)
    masks = (mine, mine2, mask, high, low, mask_share, mask_own, both_share)
    chip = turn.astype(jnp.int32)
    rows_here = ((jobs == chip).astype(BF), (jobs2 == chip).astype(BF))
    half0 = place % CORES == 0
    flags = (core == 0, half0, section == 0, section == sections - 1, chip % 2 == 0)
    columns01 = (lane == 0, lane == 1)
    owns = (jnp.where(half0, bd, bd2), jnp.where(half0, au, au2))
    aside = lax.optimization_barrier((ends, masks, flags, columns01, rows_here, owns, place, turn))
    ends, masks, flags, columns01, rows_here, owns, place, turn = aside
    core0 = flags[0]
    kept = jnp.where(core0, ends[:CHIPS], ends[CHIPS:])
    sent = jnp.where(core0, ends[CHIPS:], ends[:CHIPS])
    got = core_swap(sent)
    x, g = [
        turned(jnp.stack([kept[:, i], got[:, i]], axis=1), 0).reshape(replicas, block, width)
        for i in range(2)
    ]
    zero = jnp.uint32(0)
    x_start, g_start = [
        lax.dynamic_slice(v, (place, zero, zero), (1, block, width))[0] for v in (x, g)
    ]
    x_own, g_own = x_start, g_start
    ups = resident(LOAD_LIMITS[0], wu, wu2, au, au2)
    state = (x, g, x_start, x_own, g_start, g_own)
    ready = lax.optimization_barrier((state, ups, masks, flags, columns01, rows_here, owns))
    state, ups, masks, flags, (lane0, lane1), rows_here, owns = ready
    x, g, x_start, x_own, g_start, g_own = state
    mine, mine2, mask, high, low, mask_share, mask_own, both_share = masks
    core0, _, at_first, at_last, even = flags
    wu, wu2, au, au2 = ups

    z_shapes = [(block, hidden + fold)] * CHIPS
    dp_shape = (replicas, block, width + fold)
    parts = call(up_kernel, z_shapes, x, mine, high, low, *ups)
    others = lax.optimization_barrier((parts, wd, wd2, bd, bd2, bu, ad))
    parts, (wd, wd2, bd, bd2, bu, ad) = others[0], others[1:]
    held = resident(LOAD_LIMITS[1], wd, wd2, bd, bd2, bu, ad, *owns)
    wd, wd2, bd, bd2, bu, ad, bd_own, au_own = held

    def activate(summed):
        adapter = summed[:, hidden:]
        ss = jnp.sum(adapter * both_share, axis=1, keepdims=True)
        rs = lax.rsqrt(ss / D + EPS)
        qb = unfolded(adapter, mask_share)
        pre = summed[:, :hidden] + mm(qb, bu)
        u = rs * pre
        return rs, qb, pre, u, jax.nn.silu(u).astype(BF)

    turned_weights = {}
    for tick in range(sections - 1):
        if tick:
            parts = call(up_kernel, z_shapes, x, mine, high, low, *ups)
        act = activate(z_sum(parts))[-1]
        if not tick:
            acts = z_gather(act)
        else:
            act, *pair = lax.optimization_barrier((act, *((wu, wu2) if tick == 1 else (wd, wd2))))
            acts = z_gather(act)
            turned_weights[tick] = transposed(*pair)
            acts, turned_weights[tick] = lax.optimization_barrier((acts, turned_weights[tick]))
        y = call(down_kernel, [dp_shape], *acts, mine, wd, wd2, ad)[0]
        y = total(dp_exchange(y))
        rb = unfolded(y[:, width:], mask_own)
        h = (x_own.astype(F32) + y[:, :width] + mm(rb, bd_own)).astype(BF)
        x_own = jnp.where(at_first, x_start, pipe_shift(h, 1))
        x = dp_exchange(to_all(x_own, replicas))

    (wu_t, wu2_t), (wd_t, wd2_t) = turned_weights[1], turned_weights[2]
    downs = (wd_t, wd2_t, bd, bd2)
    shapes = [(2,) + shape for shape in z_shapes]
    summed = z_sum(call(turn_kernel, shapes, x, mine, high, low, *ups, g, *downs))
    rs, qb, pre, u, act = activate(summed[0])
    slope = silu_grad(u)
    d_sum = summed[1]

    def hidden_grads(d_sum):
        d_rb = unfolded(d_sum[:, hidden:], mask_share)
        d_u = (d_sum[:, :hidden] + mm_last(d_rb, ad)) * slope
        return d_rb, d_u, (d_u * rs).astype(BF)

    def columns(value):
        value = value.reshape(CHIPS, CORES, block, width)
        return value[:, 0].reshape(rows, width), core_swap(value[:, 1].reshape(rows, width))

    for tick in range(sections - 1):
        d_rb, d_u, d_sb = hidden_grads(d_sum)
        factor = (rs**3 / D) * jnp.sum(d_u * pre, axis=1, keepdims=True)
        top = lax.reduce_precision(factor, 8, 7)
        terms = jnp.where(lane0, top, jnp.where(lane1, factor - top, F32(0.0)))
        sent = jnp.concatenate([d_sb, terms.astype(BF)], axis=1)
        if tick == 0:
            sent, x = lax.optimization_barrier((sent, x))
            gathered, xs = lax.optimization_barrier((z_gather(sent), columns(x)))
        else:
            gathered = z_gather(sent)
        d = call(down_back_kernel, [dp_shape], *gathered, x, mine, wu_t, wu2_t, bu)[0]
        d = total(dp_exchange(d))
        d_qb = unfolded(d[:, width:], mask_own)
        d_x = g_own.astype(F32) + d[:, :width] + mm_last(d_qb, au_own)
        d_x = pipe_shift(d_x.astype(BF), -1)
        g_own = jnp.where(at_last, g_start, d_x)
        g = dp_exchange(to_all(g_own, replicas))
        d_sum = z_sum(call(up_back_kernel, z_shapes, g, mine, *downs))

    d_rb, d_u, d_sb = hidden_grads(d_sum)

    def packed(one, two):
        return jnp.concatenate([v[:, :fold] + v[:, fold:] for v in (one, two)], axis=1)

    def rows_of(values):
        value = jnp.concatenate(values, axis=0)
        return value, core_swap(value)

    g, d_sb = lax.optimization_barrier((g, d_sb))
    d_q = folded(mm_last(d_sb, bu), mine[:block])
    r = folded(mm(act, ad), mine[:block])
    sums = d_q + jnp.concatenate([r[:, RMAX:], r[:, :RMAX]], axis=1)
    sums = dp_exchange(to_all(sums.astype(BF), replicas))
    wide = z_gather(jnp.concatenate([d_sb, act, packed(qb, d_rb)], axis=1))
    sums, wide = lax.optimization_barrier((sums, wide))
    wide = rows_of(wide)
    sums = total(sums)
    swapped = jnp.concatenate([sums[:, RMAX:], sums[:, :RMAX]], axis=1)
    narrow = packed(unfolded(sums, mask_share), unfolded(swapped, mask_share))
    narrow = z_gather(narrow)

    gs = columns(g)
    piece = lanes // (CHIPS * CORES)

    def own_lanes(value, here):
        cuts = [value[:, i : i + piece] for i in range(0, fold, piece)]
        cuts = [jnp.where(core0, *pair) for pair in (cuts[:2], cuts[2:])]
        return jnp.where(even, *cuts) * here

    def outer(left, right):
        return mm_first(*[jnp.concatenate(side, axis=0) for side in (left, right)])

    qbs = [own_lanes(v[:, 2 * hidden : 2 * hidden + fold], h) for v, h in zip(wide, rows_here)]
    d_rbs = [own_lanes(v[:, 2 * hidden + fold :], h) for v, h in zip(wide, rows_here)]
    grad_bu = outer(qbs, [v[:, :hidden] for v in wide])
    grad_ad = outer([v[:, hidden : 2 * hidden] for v in wide], d_rbs)
    narrow, grad_bu, grad_ad = lax.optimization_barrier((narrow, grad_bu, grad_ad))
    both = list(zip(rows_of(narrow), (mine, mine2)))
    grad_au = outer(xs, [unfolded(v[:, :fold], m) for v, m in both])
    grad_bd = outer([unfolded(v[:, fold:], m) for v, m in both], gs)
    return (grad_au[None], grad_bu[None], grad_ad[None], grad_bd[None])


def solution(mesh):
    in_specs = (
        P(None, "dp", "tensor"),
        P(None, "dp", "tensor"),
        P("pipe", "tensor", "dp"),
        P("pipe", "dp", "tensor"),
        P("pipe", "tensor", None),
        P("pipe", None, "dp"),
        P("pipe", "dp", None),
        P("pipe", None, "tensor"),
        P(),
        P(),
    )
    out_specs = (
        P("pipe", "tensor", None),
        P("pipe", "tensor", "dp"),
        P("pipe", "dp", "tensor"),
        P("pipe", None, "tensor"),
    )
    return jax.shard_map(
        per_device, mesh=mesh, in_specs=in_specs, out_specs=out_specs, check_vma=False
    )
```
